32 devices in a mesh: grp: 1, lat: 32 (over z, y, x, core).
Axes of the slice: x: 2, y: 2, z: 4, core: 2. Of those that a mesh axis runs over, the one named last changes fastest.
Arguments:
- spectrum: bfloat16 [2688, 128, 256], P(('grp', 'lat')), may hold values from -6 to 6
- owners: int32 [384], P('lat'), may hold values from 0 to 383, each once
- legendre: bfloat16 [2688, 128, 640], P('lat'), may hold values from -0.25 to 0.25
- gauss_weights: float32 [640], replicated, may hold values from 0.5 to 2
Outputs:
- grid_values: bfloat16 [640, 2, 1536, 128], P(('grp', 'lat'))
- tendency: bfloat16 [2688, 128, 256], P(('grp', 'lat'))
The draws below stay inside these ranges and needn't reach their ends.
Inputs may be any that keep to these rules, and one draw needn't show every extreme that they name: `owners`: each pair index appears once; pair p stands for the wavenumbers p and 767 - p.
All inputs are finite; a program needn't handle non-finite values.
Results may differ from the reference program's by a relative error of at most 0.0092.
Values may be sent and summed in bfloat16 or wider, within the bound.
A program may use at most 256 MiB of HBM per device.

```python
import math
import jax
import jax.numpy as jnp
from jax import lax

M = 768
BS = 128
LATP = 640
LEV = 64
COLS = 128
NB = 6
NBP = 7
NLON = 1536


def level_of(key, dims, shards, least, top_value):
    factor_of, own = 1.0, jax.random.fold_in(key, 6)
    for dim, blocks in shards:
        steps = jnp.exp(jax.random.uniform(jax.random.fold_in(own, dim), (blocks,), jnp.float32, least / len(shards), top_value / len(shards)))
        factor_of = factor_of * jnp.repeat(steps, dims[dim] // blocks).reshape([-1 if axis == dim else 1 for axis in range(len(dims))])
    return factor_of


def scatter_about(key, extent, deviation, reach, cuts=(), kind=jnp.bfloat16):
    result = jax.random.normal(key, extent, jnp.float32) * deviation
    if len(cuts) > 0:
        result = level_of(key, extent, cuts, -0.22, 0.18) * result
    return jnp.clip(result, min=-reach, max=reach).astype(kind)


def setup_inputs(seed: int = 0, part: int = 0) -> dict:
    seeds = jax.random.split(jax.random.key(seed), 5)
    part_splits = jax.random.split(jax.random.fold_in(seeds[4], part), 5)
    spectrum = scatter_about(part_splits[0], (M // 2 * NBP, BS, 2 * COLS), 1.0, 6.0, ((0, 32),))
    owners = jax.random.permutation(seeds[1], M // 2).astype(jnp.int32)
    legendre = scatter_about(seeds[2], (M // 2 * NBP, BS, LATP), LATP ** -0.5, 0.25, ((0, 32),))
    gauss_weights = jnp.clip(jnp.exp(jax.random.uniform(seeds[3], (LATP,), jnp.float32, math.log(0.5), math.log(2.0))), 0.5, 2.0)
    return {"spectrum": spectrum, "owners": owners, "legendre": legendre, "gauss_weights": gauss_weights}


def block_layout(pair_ids):
    lowest = pair_ids // BS
    block_ids = jnp.arange(NBP, dtype=jnp.int32)
    leading = block_ids[None, :] < (NB - lowest)[:, None]
    wavenum = jnp.where(leading, pair_ids[:, None], M - 1 - pair_ids[:, None])
    nblock = jnp.where(leading, lowest[:, None] + block_ids[None, :], block_ids[None, :] - 1)
    half_rows = BS // 2
    row_ids = jnp.arange(BS, dtype=jnp.int32)
    odd_flag = (row_ids >= half_rows).astype(jnp.int32)
    degree = nblock[:, :, None] * BS + 2 * (row_ids % half_rows)[None, None, :] + (wavenum[:, :, None] + odd_flag[None, None, :]) % 2
    live_rows = degree >= wavenum[:, :, None]
    return (leading, live_rows)

def fourier_basis(pair_ids):
    wave_list = jnp.stack([pair_ids, M - 1 - pair_ids], axis=1).reshape(M).astype(jnp.int32)
    longitude = jnp.arange(NLON, dtype=jnp.int32)
    phase_idx = longitude[:, None] * wave_list[None, :] % NLON
    angles = phase_idx.astype(jnp.float32) * (2.0 * math.pi / NLON)
    scaled = jnp.stack([jnp.cos(angles), -jnp.sin(angles)], axis=-1) * (1.0 / math.sqrt(M))
    return scaled.astype(jnp.bfloat16).reshape(NLON, 2 * M)

def reference(spectrum, owners, legendre, gauss_weights):
    half_rows = BS // 2
    leading, live_rows = block_layout(owners)
    spec_four = spectrum.reshape(M // 2, NBP, BS, 2 * COLS)
    table_four = legendre.reshape(M // 2, NBP, BS, LATP)

    def inverse_pair(pieces):
        spec_pair, table_pair, lead_pair, live_pair = pieces
        masked = spec_pair * live_pair[:, :, None].astype(jnp.bfloat16)
        table_wide = table_pair.astype(jnp.float32)
        masked_wide = masked.astype(jnp.float32)
        even_part = jnp.einsum('jrl,jrc->jlc', table_wide[:, :half_rows], masked_wide[:, :half_rows])
        odd_part = jnp.einsum('jrl,jrc->jlc', table_wide[:, half_rows:], masked_wide[:, half_rows:])
        weight_one = lead_pair.astype(jnp.float32)[:, None, None]
        symmetric = jnp.stack([lax.optimization_barrier(jnp.sum(even_part * weight_one, 0)), lax.optimization_barrier(jnp.sum(even_part * (1.0 - weight_one), 0))], 0)
        antisym = jnp.stack([lax.optimization_barrier(jnp.sum(odd_part * weight_one, 0)), lax.optimization_barrier(jnp.sum(odd_part * (1.0 - weight_one), 0))], 0)
        return jnp.stack([symmetric + antisym, symmetric - antisym], axis=2).astype(jnp.bfloat16)
    fourier = lax.map(inverse_pair, (spec_four, table_four, leading, live_rows))
    fourier = fourier.reshape(M, LATP, 2, 2, COLS).transpose(1, 2, 0, 3, 4)
    fourier_table = fourier_basis(owners).astype(jnp.float32)

    def grid_row(fourier_row):
        flattened = fourier_row.reshape(2, 2 * M, COLS).astype(jnp.float32)
        values = jnp.einsum('wk,hkc->hwc', fourier_table, flattened)
        wind_u = values[..., :LEV]
        wind_v = values[..., LEV:]
        product = jnp.concatenate([wind_u * wind_v, 0.5 * (wind_u * wind_u - wind_v * wind_v)], axis=-1).astype(jnp.bfloat16)
        coeffs = jnp.einsum('wk,hwc->hkc', fourier_table, product.astype(jnp.float32)).astype(jnp.bfloat16)
        return (values.astype(jnp.bfloat16), coeffs.reshape(2, M, 2, COLS))
    grid_values, returned = lax.map(grid_row, fourier)
    weights = gauss_weights[:, None, None, None]
    returned_wide = returned.astype(jnp.float32)
    symmetric = (weights * (returned_wide[:, 0] + returned_wide[:, 1])).astype(jnp.bfloat16)
    antisym = (weights * (returned_wide[:, 0] - returned_wide[:, 1])).astype(jnp.bfloat16)
    sym_pairs = symmetric.reshape(LATP, M // 2, 2, 2 * COLS).transpose(1, 2, 0, 3)
    anti_pairs = antisym.reshape(LATP, M // 2, 2, 2 * COLS).transpose(1, 2, 0, 3)

    def direct_pair(pieces):
        table_pair, lead_pair, live_pair, sym_pair, anti_pair = pieces
        chosen_sym = jnp.where(lead_pair[:, None, None], sym_pair[0][None], sym_pair[1][None]).astype(jnp.float32)
        chosen_anti = jnp.where(lead_pair[:, None, None], anti_pair[0][None], anti_pair[1][None]).astype(jnp.float32)
        table_wide = table_pair.astype(jnp.float32)
        even_rows = jnp.einsum('jrl,jlc->jrc', table_wide[:, :half_rows], chosen_sym)
        odd_rows = jnp.einsum('jrl,jlc->jrc', table_wide[:, half_rows:], chosen_anti)
        combined = jnp.concatenate([even_rows, odd_rows], axis=1) * live_pair[:, :, None].astype(jnp.float32)
        return combined.astype(jnp.bfloat16)
    tendency = lax.map(direct_pair, (table_four, leading, live_rows, sym_pairs, anti_pairs))
    return (grid_values, tendency.reshape(M // 2 * NBP, BS, 2 * COLS))
```

```python
import functools
import math

import jax
import jax.numpy as jnp
from jax import lax
from jax.experimental import pallas as pl
from jax.experimental.pallas import tpu as pltpu
from jax.sharding import PartitionSpec as P

BF = jnp.bfloat16
F32 = jnp.float32
CHUNKS = 5


def dot(a, b, dims):
    return lax.dot_general(a, b, (dims, ((), ())), preferred_element_type=F32)


def params(mib):
    return pltpu.CompilerParams(vmem_limit_bytes=mib * 1024 * 1024)


def block_facts(p, j, nb, bs, m_count, shape):
    k = p // bs
    lead = j < nb - k
    m = jnp.where(lead, p, m_count - 1 - p)
    b = jnp.where(lead, k + j, j - 1)
    r = lax.broadcasted_iota(jnp.int32, shape, 0)
    half = bs // 2
    odd = (r >= half).astype(jnp.int32)
    degree = b * bs + 2 * (r % half) + ((m + odd) & 1)
    return lead, degree >= m


def inverse_kernel(dims, owners_ref, leg_ref, spec_ref, out_ref, acc_ref):
    nbp, bs, nb, m_count, rows, stride, chan = dims
    q = pl.program_id(0)
    half = bs // 2
    p = owners_ref[q]
    firsts, seconds = [], []
    for j in range(nbp):
        s = spec_ref[j].astype(F32)
        lead, live = block_facts(p, j, nb, bs, m_count, s.shape)
        one = lead.astype(F32)
        s = jnp.where(live, s, 0.0)
        both = jnp.concatenate([s * one, s * (1.0 - one)], axis=1).astype(BF)
        firsts.append(both[:half])
        seconds.append(both[half:])
    te = jnp.concatenate([leg_ref[j, :half] for j in range(nbp)], axis=0)
    to = jnp.concatenate([leg_ref[j, half:] for j in range(nbp)], axis=0)
    sym = dot(te, jnp.concatenate(firsts, axis=0), ((0,), (0,)))
    anti = dot(to, jnp.concatenate(seconds, axis=0), ((0,), (0,)))
    lats = sym.shape[0]
    for h, val in enumerate((sym + anti, sym - anti)):
        for x in range(4):
            acc_ref[h, pl.ds(q * 4 + x, lats, stride=stride), :] = val[:, x * chan:(x + 1) * chan]

    @pl.when(q == pl.num_programs(0) - 1)
    def _():
        for h in range(2):
            full = acc_ref[h].reshape(lats, stride, chan)
            out_ref[:, :, h * chan:(h + 1) * chan] = full[:, :rows].astype(BF)


def inverse(owners, leg, spec, chunk, lats, dims):
    nbp, bs, nb, m_count, rows, stride, chan = dims
    pairs = owners.shape[0]
    return pl.pallas_call(
        functools.partial(inverse_kernel, dims),
        grid_spec=pltpu.PrefetchScalarGridSpec(
            num_scalar_prefetch=1,
            grid=(pairs,),
            in_specs=[
                pl.BlockSpec((nbp, bs, lats), lambda q, o: (q, 0, chunk)),
                pl.BlockSpec((nbp, bs, 2 * chan), lambda q, o: (q, 0, 0)),
            ],
            out_specs=pl.BlockSpec((lats, rows, 2 * chan), lambda q, o: (0, 0, 0)),
            scratch_shapes=[pltpu.VMEM((2, lats * stride, chan), F32)],
        ),
        out_shape=jax.ShapeDtypeStruct((lats, rows, 2 * chan), BF),
        compiler_params=params(48),
        cost_estimate=pl.CostEstimate(flops=4 * 10**9, bytes_accessed=15 * 10**6, transcendentals=0),
        name="inverse_legendre",
    )(owners, leg, spec)


def fourier_kernel(chan, table_ref, turned_ref, recv_ref, prev_ref, grid_ref, send_ref):
    groups, _, rows, cols = recv_ref.shape
    total = groups * rows
    f = recv_ref[:, 0].reshape(total, cols)
    nlon = table_ref.shape[0]
    step = nlon // 4
    fluxes = []
    for w in range(4):
        values = dot(table_ref[w * step:(w + 1) * step], f, ((1,), (0,)))
        parts = []
        for h in range(2):
            x = values[:, h * chan:(h + 1) * chan]
            grid_ref[0, h, w * step:(w + 1) * step, :] = x.astype(BF)
            y = pltpu.roll(x, chan // 2, 1)
            lane = lax.broadcasted_iota(jnp.int32, x.shape, 1)
            parts.append(jnp.where(lane < chan // 2, x * y, 0.5 * (y * y - x * x)).astype(BF))
        fluxes.append(jnp.concatenate(parts, axis=1))
    flux = jnp.concatenate(fluxes, axis=0)
    coeffs = dot(turned_ref[...], flux, ((1,), (0,))).astype(BF)
    send_ref[:, 0] = coeffs.reshape(groups, rows, cols)


def fourier(table, turned, recv, prev, chunk, grid_shape):
    groups, lats, rows, cols = recv.shape
    nlon, total = table.shape
    chan = cols // 2
    whole = pl.BlockSpec((nlon, total), lambda t: (0, 0))
    turned_spec = pl.BlockSpec((total, nlon), lambda t: (0, 0))
    part = pl.BlockSpec((groups, 1, rows, cols), lambda t: (0, t, 0, 0))
    in_specs = [whole, turned_spec, part]
    args = [table, turned, recv]
    kernel = functools.partial(fourier_kernel, chan)
    alias = {}
    if prev is None:
        def kernel(a, b, c, d, e):
            fourier_kernel(chan, a, b, c, None, d, e)
    else:
        in_specs.append(pl.BlockSpec(memory_space=pl.ANY))
        args.append(prev)
        alias = {3: 0}
    return pl.pallas_call(
        kernel,
        grid=(lats,),
        in_specs=in_specs,
        out_specs=[
            pl.BlockSpec((1, 2, nlon, chan), lambda t: (chunk * lats + t, 0, 0, 0)),
            part,
        ],
        out_shape=[
            jax.ShapeDtypeStruct(grid_shape, BF),
            jax.ShapeDtypeStruct(recv.shape, BF),
        ],
        input_output_aliases=alias,
        compiler_params=params(56),
        cost_estimate=pl.CostEstimate(flops=4 * lats * nlon * total * cols, bytes_accessed=20 * 10**6, transcendentals=0),
        name="fourier_step",
    )(*args)


def direct_kernel(dims, first, last, owners_ref, leg_ref, gauss_ref, got_ref, *rest):
    nbp, bs, nb, m_count, rows, stride, chan = dims
    prev_ref = None if first else rest[0]
    out_ref, acc_ref = rest[-2:]
    q = pl.program_id(0)
    half = bs // 2
    p = owners_ref[q]
    lats = got_ref.shape[0]

    @pl.when(q == 0)
    def _():
        for h in range(2):
            full = got_ref[:, :, h * chan:(h + 1) * chan].astype(F32)
            if stride != rows:
                full = jnp.concatenate([full, jnp.zeros((lats, stride - rows, chan), F32)], axis=1)
            acc_ref[h] = full.reshape(lats * stride, chan)

    g = gauss_ref[...]
    syms, antis = [], []
    for x in range(4):
        north = acc_ref[0, pl.ds(q * 4 + x, lats, stride=stride), :]
        south = acc_ref[1, pl.ds(q * 4 + x, lats, stride=stride), :]
        syms.append((g * (north + south)).astype(BF))
        antis.append((g * (north - south)).astype(BF))
    te = jnp.concatenate([leg_ref[j, :half] for j in range(nbp)], axis=0)
    to = jnp.concatenate([leg_ref[j, half:] for j in range(nbp)], axis=0)
    even = dot(te, jnp.concatenate(syms, axis=1), ((1,), (0,)))
    odd = dot(to, jnp.concatenate(antis, axis=1), ((1,), (0,)))
    for j in range(nbp):
        both = jnp.concatenate([even[j * half:(j + 1) * half], odd[j * half:(j + 1) * half]], axis=0)
        shape = (bs, 2 * chan)
        lead, live = block_facts(p, j, nb, bs, m_count, shape)
        one = lead.astype(jnp.int32)
        pick = jnp.where(jnp.broadcast_to(one, shape) == 1, both[:, :2 * chan], both[:, 2 * chan:])
        if not first:
            pick = pick + prev_ref[j]
        if last:
            pick = jnp.where(live, pick, 0.0)
        out_ref[j] = pick.astype(out_ref.dtype)


def direct(owners, leg, gauss, got, prev, chunk, dims, last):
    nbp, bs, nb, m_count, rows, stride, chan = dims
    pairs = owners.shape[0]
    lats = got.shape[0]
    blocks = pl.BlockSpec((nbp, bs, 2 * chan), lambda q, o: (q, 0, 0))
    in_specs = [
        pl.BlockSpec((nbp, bs, lats), lambda q, o: (q, 0, chunk)),
        pl.BlockSpec((lats, chan), lambda q, o: (chunk, 0)),
        pl.BlockSpec((lats, rows, 2 * chan), lambda q, o: (0, 0, 0)),
    ]
    args = [owners, leg, gauss, got]
    alias = {}
    if prev is not None:
        in_specs.append(blocks)
        args.append(prev)
        if not last:
            alias = {4: 0}
    return pl.pallas_call(
        functools.partial(direct_kernel, dims, prev is None, last),
        grid_spec=pltpu.PrefetchScalarGridSpec(
            num_scalar_prefetch=1,
            grid=(pairs,),
            in_specs=in_specs,
            out_specs=blocks,
            scratch_shapes=[pltpu.VMEM((2, lats * stride, chan), F32)],
        ),
        out_shape=jax.ShapeDtypeStruct((pairs * nbp, bs, 2 * chan), BF if last else F32),
        input_output_aliases=alias,
        compiler_params=params(48),
        cost_estimate=pl.CostEstimate(flops=4 * 10**9, bytes_accessed=30 * 10**6, transcendentals=0),
        name="direct_legendre",
    )(*args)


def fourier_basis(pair_ids, m_count, nlon):
    wave = jnp.stack([pair_ids, m_count - 1 - pair_ids], axis=1).reshape(m_count, 1)
    longitude = jnp.arange(nlon, dtype=jnp.int32)[None, :]
    angles = (longitude * wave % nlon).astype(F32) * (2.0 * math.pi / nlon)
    scaled = jnp.stack([jnp.cos(angles), -jnp.sin(angles)], axis=1) * (1.0 / math.sqrt(m_count))
    return scaled.astype(BF).reshape(2 * m_count, nlon)


def per_device(spectrum, owners, legendre, gauss_weights):
    pairs = owners.shape[0]
    devices = lax.axis_size("lat")
    blocks, bs, cols = spectrum.shape
    nbp = blocks // pairs
    nb = nbp - 1
    chan = cols // 2
    m_count = 2 * pairs * devices
    nlon = 2 * m_count
    latp = legendre.shape[2]
    here = latp // devices
    chunks = CHUNKS if here % CHUNKS == 0 else 1
    tc = here // chunks
    lats = devices * tc
    rows = 4 * pairs
    stride = -(-rows // 16) * 16
    dims = (nbp, bs, nb, m_count, rows, stride, chan)

    all_owners = lax.all_gather(owners, "lat", axis=0, tiled=True)
    mine = lax.dynamic_slice(all_owners, (lax.axis_index("lat") * pairs,), (pairs,))

    place = jnp.arange(latp, dtype=jnp.int32).reshape(devices, chunks, tc).transpose(1, 0, 2).reshape(latp)
    onehot = (jnp.arange(latp, dtype=jnp.int32)[:, None] == place[None, :]).astype(BF)
    leg = jnp.dot(legendre.reshape(blocks * bs, latp), onehot, preferred_element_type=F32).astype(BF)
    leg = leg.reshape(blocks, bs, latp)
    gauss = gauss_weights.reshape(devices, chunks, tc).transpose(1, 0, 2).reshape(latp, 1)
    gauss = jnp.broadcast_to(gauss, (latp, chan))

    received = []
    for c in range(chunks):
        out = inverse(mine, leg, spectrum, c, lats, dims)
        out = out.reshape(devices, tc, rows, cols)
        received.append(lax.all_to_all(out, "lat", split_axis=0, concat_axis=0, tiled=True))

    turned = fourier_basis(all_owners, m_count, nlon)
    table = turned.T
    grid = None
    tendency = None
    aligned = rows % 16 == 0
    grid_shape = (here, 2, nlon, chan)
    arrived = []
    for c in range(chunks):
        got = received[c]
        if not aligned:
            got = got.transpose(1, 0, 2, 3).reshape(1, tc, devices * rows, cols)
        grid, send = fourier(table, turned, got, grid, c, grid_shape)
        if not aligned:
            send = send.reshape(tc, devices, rows, cols).transpose(1, 0, 2, 3)
        arrived.append(lax.all_to_all(send, "lat", split_axis=0, concat_axis=0, tiled=True))
    for c in range(chunks):
        got = arrived[c].reshape(lats, rows, cols)
        tendency = direct(mine, leg, gauss, got, tendency, c, dims, c == chunks - 1)
    return grid, tendency


def solution(mesh):
    in_specs = (P(("grp", "lat"), None, None), P("lat"), P("lat", None, None), P())
    out_specs = (P(("grp", "lat"), None, None, None), P(("grp", "lat"), None, None))
    return jax.shard_map(
        per_device, mesh=mesh, in_specs=in_specs, out_specs=out_specs, check_vma=False
    )
```

```python
import functools
import math

import jax
import jax.numpy as jnp
from jax import lax
from jax.experimental import pallas as pl
from jax.experimental.pallas import tpu as pltpu
from jax.sharding import PartitionSpec as P

BF = jnp.bfloat16
F32 = jnp.float32


def dot(a, b, dims):
    return lax.dot_general(a, b, (dims, ((), ())), preferred_element_type=F32)


def params(mib):
    return pltpu.CompilerParams(vmem_limit_bytes=mib * 1024 * 1024)


def block_facts(p, j, nb, bs, m_count, shape):
    k = p // bs
    lead = j < nb - k
    m = jnp.where(lead, p, m_count - 1 - p)
    b = jnp.where(lead, k + j, j - 1)
    r = lax.broadcasted_iota(jnp.int32, shape, 0)
    half = bs // 2
    odd = (r >= half).astype(jnp.int32)
    degree = b * bs + 2 * (r % half) + ((m + odd) & 1)
    return lead, degree >= m


def inverse_kernel(dims, owners_ref, leg_ref, spec_ref, order_ref, out_ref, table_ref, acc_ref):
    nbp, bs, nb, m_count, rows, stride, chan = dims
    q = pl.program_id(0)
    half = bs // 2
    p = owners_ref[q]
    firsts, seconds = [], []
    for j in range(nbp):
        s = spec_ref[j].astype(F32)
        lead, live = block_facts(p, j, nb, bs, m_count, s.shape)
        one = lead.astype(F32)
        s = jnp.where(live, s, 0.0)
        both = jnp.concatenate([s * one, s * (1.0 - one)], axis=1).astype(BF)
        firsts.append(both[:half])
        seconds.append(both[half:])
    picked = dot(leg_ref[...].reshape(nbp * bs, leg_ref.shape[2]), order_ref[...], ((1,), (0,))).astype(BF)
    table_ref[...] = picked.reshape(table_ref.shape)
    te = jnp.concatenate([picked[j * bs:j * bs + half] for j in range(nbp)], axis=0)
    to = jnp.concatenate([picked[j * bs + half:(j + 1) * bs] for j in range(nbp)], axis=0)
    sym = dot(te, jnp.concatenate(firsts, axis=0), ((0,), (0,)))
    anti = dot(to, jnp.concatenate(seconds, axis=0), ((0,), (0,)))
    lats = sym.shape[0]
    for h, val in enumerate((sym + anti, sym - anti)):
        for x in range(4):
            acc_ref[h, pl.ds(q * 4 + x, lats, stride=stride), :] = val[:, x * chan:(x + 1) * chan]

    @pl.when(q == pl.num_programs(0) - 1)
    def _():
        def move(i, _):
            for h in range(2):
                full = acc_ref[h, pl.ds(i * 16 * stride, 16 * stride), :].reshape(16, stride, chan)
                out_ref[pl.ds(i * 16, 16), :, h * chan:(h + 1) * chan] = full[:, :rows].astype(BF)
            return 0

        lax.fori_loop(0, lats // 16, move, 0)


def inverse(owners, leg, spec, order, dims):
    nbp, bs, nb, m_count, rows, stride, chan = dims
    pairs = owners.shape[0]
    latp, lats = order.shape
    return pl.pallas_call(
        functools.partial(inverse_kernel, dims),
        grid_spec=pltpu.PrefetchScalarGridSpec(
            num_scalar_prefetch=1,
            grid=(pairs,),
            in_specs=[
                pl.BlockSpec((nbp, bs, latp), lambda q, o: (q, 0, 0)),
                pl.BlockSpec((nbp, bs, 2 * chan), lambda q, o: (q, 0, 0)),
                pl.BlockSpec((latp, lats), lambda q, o: (0, 0)),
            ],
            out_specs=[
                pl.BlockSpec((lats, rows, 2 * chan), lambda q, o: (0, 0, 0)),
                pl.BlockSpec((nbp, bs, lats), lambda q, o: (q, 0, 0)),
            ],
            scratch_shapes=[pltpu.VMEM((2, lats * stride, chan), F32)],
        ),
        out_shape=[
            jax.ShapeDtypeStruct((lats, rows, 2 * chan), BF),
            jax.ShapeDtypeStruct((pairs * nbp, bs, lats), BF),
        ],
        compiler_params=params(58),
        cost_estimate=pl.CostEstimate(
            flops=lats * 90 * 10**6, bytes_accessed=20 * 10**6 + lats * 10**5, transcendentals=0
        ),
        name="inverse_legendre",
    )(owners, leg, spec, order)


def fourier_kernel(chan, table_ref, turned_ref, recv_ref, prev_ref, grid_ref, send_ref):
    groups, _, rows, cols = recv_ref.shape
    total = groups * rows
    f = recv_ref[:, 0].reshape(total, cols)
    nlon = table_ref.shape[0]
    step = nlon // 4
    fluxes = []
    for w in range(4):
        values = dot(table_ref[w * step:(w + 1) * step], f, ((1,), (0,)))
        parts = []
        for h in range(2):
            x = values[:, h * chan:(h + 1) * chan]
            grid_ref[0, h, w * step:(w + 1) * step, :] = x.astype(BF)
            y = pltpu.roll(x, chan // 2, 1)
            lane = lax.broadcasted_iota(jnp.int32, x.shape, 1)
            parts.append(jnp.where(lane < chan // 2, x * y, 0.5 * (y * y - x * x)).astype(BF))
        fluxes.append(jnp.concatenate(parts, axis=1))
    flux = jnp.concatenate(fluxes, axis=0)
    coeffs = dot(turned_ref[...], flux, ((1,), (0,))).astype(BF)
    send_ref[:, 0] = coeffs.reshape(groups, rows, cols)


def fourier(table, turned, recv, prev, start, grid_shape):
    groups, lats, rows, cols = recv.shape
    nlon, total = table.shape
    chan = cols // 2
    whole = pl.BlockSpec((nlon, total), lambda t: (0, 0))
    turned_spec = pl.BlockSpec((total, nlon), lambda t: (0, 0))
    part = pl.BlockSpec((groups, 1, rows, cols), lambda t: (0, t, 0, 0))
    in_specs = [whole, turned_spec, part]
    args = [table, turned, recv]
    kernel = functools.partial(fourier_kernel, chan)
    alias = {}
    if prev is None:
        def kernel(a, b, c, d, e):
            fourier_kernel(chan, a, b, c, None, d, e)
    else:
        in_specs.append(pl.BlockSpec(memory_space=pl.ANY))
        args.append(prev)
        alias = {3: 0}
    return pl.pallas_call(
        kernel,
        grid=(lats,),
        in_specs=in_specs,
        out_specs=[
            pl.BlockSpec((1, 2, nlon, chan), lambda t: (start + t, 0, 0, 0)),
            part,
        ],
        out_shape=[
            jax.ShapeDtypeStruct(grid_shape, BF),
            jax.ShapeDtypeStruct(recv.shape, BF),
        ],
        input_output_aliases=alias,
        compiler_params=params(56),
        cost_estimate=pl.CostEstimate(flops=4 * lats * nlon * total * cols, bytes_accessed=20 * 10**6, transcendentals=0),
        name="fourier_step",
    )(*args)


def direct_kernel(dims, first, last, owners_ref, leg_ref, gauss_ref, got_ref, *rest):
    nbp, bs, nb, m_count, rows, stride, chan = dims
    prev_ref = None if first else rest[0]
    out_ref, acc_ref = rest[-2:]
    q = pl.program_id(0)
    half = bs // 2
    p = owners_ref[q]
    lats = got_ref.shape[0]

    @pl.when(q == 0)
    def _():
        def move(i, _):
            for h in range(2):
                full = got_ref[pl.ds(i * 16, 16), :, h * chan:(h + 1) * chan].astype(F32)
                if stride != rows:
                    full = jnp.concatenate([full, jnp.zeros((16, stride - rows, chan), F32)], axis=1)
                acc_ref[h, pl.ds(i * 16 * stride, 16 * stride), :] = full.reshape(16 * stride, chan)
            return 0

        lax.fori_loop(0, lats // 16, move, 0)

    g = gauss_ref[...]
    syms, antis = [], []
    for x in range(4):
        north = acc_ref[0, pl.ds(q * 4 + x, lats, stride=stride), :]
        south = acc_ref[1, pl.ds(q * 4 + x, lats, stride=stride), :]
        syms.append((g * (north + south)).astype(BF))
        antis.append((g * (north - south)).astype(BF))
    te = jnp.concatenate([leg_ref[j, :half] for j in range(nbp)], axis=0)
    to = jnp.concatenate([leg_ref[j, half:] for j in range(nbp)], axis=0)
    even = dot(te, jnp.concatenate(syms, axis=1), ((1,), (0,)))
    odd = dot(to, jnp.concatenate(antis, axis=1), ((1,), (0,)))
    for j in range(nbp):
        both = jnp.concatenate([even[j * half:(j + 1) * half], odd[j * half:(j + 1) * half]], axis=0)
        shape = (bs, 2 * chan)
        lead, live = block_facts(p, j, nb, bs, m_count, shape)
        one = lead.astype(jnp.int32)
        pick = jnp.where(jnp.broadcast_to(one, shape) == 1, both[:, :2 * chan], both[:, 2 * chan:])
        if not first:
            pick = pick + prev_ref[j]
        if last:
            pick = jnp.where(live, pick, 0.0)
        out_ref[j] = pick.astype(out_ref.dtype)


def direct(owners, leg, gauss, got, prev, dims, last):
    nbp, bs, nb, m_count, rows, stride, chan = dims
    pairs = owners.shape[0]
    lats = got.shape[0]
    blocks = pl.BlockSpec((nbp, bs, 2 * chan), lambda q, o: (q, 0, 0))
    in_specs = [
        pl.BlockSpec((nbp, bs, lats), lambda q, o: (q, 0, 0)),
        pl.BlockSpec((lats, chan), lambda q, o: (0, 0)),
        pl.BlockSpec((lats, rows, 2 * chan), lambda q, o: (0, 0, 0)),
    ]
    args = [owners, leg, gauss, got]
    alias = {}
    if prev is not None:
        in_specs.append(blocks)
        args.append(prev)
        if not last:
            alias = {4: 0}
    return pl.pallas_call(
        functools.partial(direct_kernel, dims, prev is None, last),
        grid_spec=pltpu.PrefetchScalarGridSpec(
            num_scalar_prefetch=1,
            grid=(pairs,),
            in_specs=in_specs,
            out_specs=blocks,
            scratch_shapes=[pltpu.VMEM((2, lats * stride, chan), F32)],
        ),
        out_shape=jax.ShapeDtypeStruct((pairs * nbp, bs, 2 * chan), BF if last else F32),
        input_output_aliases=alias,
        compiler_params=params(58),
        cost_estimate=pl.CostEstimate(
            flops=lats * 40 * 10**6, bytes_accessed=25 * 10**6 + lats * 10**5, transcendentals=0
        ),
        name="direct_legendre",
    )(*args)


def fourier_basis(pair_ids, m_count, nlon):
    wave = jnp.stack([pair_ids, m_count - 1 - pair_ids], axis=1).reshape(m_count, 1)
    longitude = jnp.arange(nlon, dtype=jnp.int32)[None, :]
    angles = (longitude * wave % nlon).astype(F32) * (2.0 * math.pi / nlon)
    scaled = jnp.stack([jnp.cos(angles), -jnp.sin(angles)], axis=1) * (1.0 / math.sqrt(m_count))
    return scaled.astype(BF).reshape(2 * m_count, nlon)


def per_device(spectrum, owners, legendre, gauss_weights):
    pairs = owners.shape[0]
    devices = lax.axis_size("lat")
    blocks, bs, cols = spectrum.shape
    nbp = blocks // pairs
    nb = nbp - 1
    chan = cols // 2
    m_count = 2 * pairs * devices
    nlon = 2 * m_count
    latp = legendre.shape[2]
    here = latp // devices
    fifth = here // 5
    sizes = (fifth, 3 * fifth, fifth) if here % 5 == 0 else (here,)
    starts = [sum(sizes[:c]) for c in range(len(sizes))]
    rows = 4 * pairs
    stride = -(-rows // 16) * 16
    dims = (nbp, bs, nb, m_count, rows, stride, chan)
    aligned = rows % 16 == 0
    grid_shape = (here, 2, nlon, chan)

    copies = jnp.broadcast_to(owners[None, :], (devices, pairs))
    all_owners = lax.all_to_all(copies, "lat", split_axis=0, concat_axis=0, tiled=True).reshape(-1)

    def swap(x):
        return lax.all_to_all(x, "lat", split_axis=0, concat_axis=0, tiled=True)

    def places(c):
        device = jnp.arange(devices, dtype=jnp.int32)[:, None]
        return (device * here + starts[c] + jnp.arange(sizes[c], dtype=jnp.int32)[None, :]).reshape(-1)

    def inverse_chunk(c):
        order = (jnp.arange(latp, dtype=jnp.int32)[:, None] == places(c)[None, :]).astype(BF)
        out, leg = inverse(owners, legendre, spectrum, order, dims)
        return out.reshape(devices, sizes[c], rows, cols), leg

    def fourier_chunk(c, got, grid):
        if not aligned:
            got = got.transpose(1, 0, 2, 3).reshape(1, sizes[c], devices * rows, cols)
        grid, send = fourier(table, turned, got, grid, starts[c], grid_shape)
        if not aligned:
            send = send.reshape(sizes[c], devices, rows, cols).transpose(1, 0, 2, 3)
        return grid, send

    count = len(sizes)
    outs, legs = zip(*[inverse_chunk(c) for c in range(count)])
    outs = list(outs)
    outs[0], all_owners = lax.optimization_barrier((outs[0], all_owners))
    received = [swap(outs[0])]
    turned = fourier_basis(all_owners, m_count, nlon)
    table = turned.T
    grid, send = fourier_chunk(0, received[0], None)
    sends = [send]
    for c in range(1, count):
        if c == 2:
            outs[c], sends[0], grid = lax.optimization_barrier((outs[c], sends[0], grid))
        received.append(swap(outs[c]))
        if c == 1:
            sends[0], received[1] = lax.optimization_barrier((sends[0], received[1]))
    for c in range(1, count):
        grid, send = fourier_chunk(c, received[c], grid)
        sends.append(send)
    tendency = None
    for c in range(count):
        got = swap(sends[c]).reshape(devices * sizes[c], rows, cols)
        gauss = jnp.broadcast_to(
            gauss_weights.reshape(devices, here)[:, starts[c]:starts[c] + sizes[c]].reshape(-1, 1),
            (devices * sizes[c], chan),
        )
        tendency = direct(owners, legs[c], gauss, got, tendency, dims, c == count - 1)
    return grid, tendency


def solution(mesh):
    in_specs = (P(("grp", "lat"), None, None), P("lat"), P("lat", None, None), P())
    out_specs = (P(("grp", "lat"), None, None, None), P(("grp", "lat"), None, None))
    return jax.shard_map(
        per_device, mesh=mesh, in_specs=in_specs, out_specs=out_specs, check_vma=False
    )
```

```python
import functools
import math

import jax
import jax.numpy as jnp
from jax import lax
from jax.experimental import pallas as pl
from jax.experimental.pallas import tpu as pltpu
from jax.sharding import PartitionSpec as P

BF = jnp.bfloat16
F32 = jnp.float32


def dot(a, b, dims):
    return lax.dot_general(a, b, (dims, ((), ())), preferred_element_type=F32)


def params(mib):
    return pltpu.CompilerParams(vmem_limit_bytes=mib * 1024 * 1024)


def block_facts(p, j, nb, bs, m_count, shape):
    k = p // bs
    lead = j < nb - k
    m = jnp.where(lead, p, m_count - 1 - p)
    b = jnp.where(lead, k + j, j - 1)
    r = lax.broadcasted_iota(jnp.int32, shape, 0)
    half = bs // 2
    odd = (r >= half).astype(jnp.int32)
    degree = b * bs + 2 * (r % half) + ((m + odd) & 1)
    return lead, degree >= m


def inverse_kernel(dims, owners_ref, leg_ref, spec_ref, order_ref, out_ref, table_ref, acc_ref):
    nbp, bs, nb, m_count, rows, stride, chan = dims
    q = pl.program_id(0)
    half = bs // 2
    p = owners_ref[q]
    firsts, seconds = [], []
    for j in range(nbp):
        s = spec_ref[j].astype(F32)
        lead, live = block_facts(p, j, nb, bs, m_count, (bs, 1))
        one = lead.astype(F32)
        keep = live.astype(F32)
        both = jnp.concatenate([s * (keep * one), s * (keep * (1.0 - one))], axis=1).astype(BF)
        firsts.append(both[:half])
        seconds.append(both[half:])
    picked = dot(leg_ref[...].reshape(nbp * bs, leg_ref.shape[2]), order_ref[...], ((1,), (0,))).astype(BF)
    table_ref[...] = picked.reshape(table_ref.shape)
    te = jnp.concatenate([picked[j * bs:j * bs + half] for j in range(nbp)], axis=0)
    to = jnp.concatenate([picked[j * bs + half:(j + 1) * bs] for j in range(nbp)], axis=0)
    sym = dot(te, jnp.concatenate(firsts, axis=0), ((0,), (0,)))
    anti = dot(to, jnp.concatenate(seconds, axis=0), ((0,), (0,)))
    lats = sym.shape[0]
    for h, val in enumerate((sym + anti, sym - anti)):
        for x in range(4):
            acc_ref[h, pl.ds(q * 4 + x, lats, stride=stride), :] = val[:, x * chan:(x + 1) * chan]

    @pl.when(q == pl.num_programs(0) - 1)
    def _():
        def move(i, _):
            for h in range(2):
                full = acc_ref[h, pl.ds(i * 16 * stride, 16 * stride), :].reshape(16, stride, chan)
                out_ref[pl.ds(i * 16, 16), :, h * chan:(h + 1) * chan] = full[:, :rows].astype(BF)
            return 0

        lax.fori_loop(0, lats // 16, move, 0)


def inverse(owners, leg, spec, order, dims):
    nbp, bs, nb, m_count, rows, stride, chan = dims
    pairs = owners.shape[0]
    latp, lats = order.shape
    return pl.pallas_call(
        functools.partial(inverse_kernel, dims),
        grid_spec=pltpu.PrefetchScalarGridSpec(
            num_scalar_prefetch=1,
            grid=(pairs,),
            in_specs=[
                pl.BlockSpec((nbp, bs, latp), lambda q, o: (q, 0, 0)),
                pl.BlockSpec((nbp, bs, 2 * chan), lambda q, o: (q, 0, 0)),
                pl.BlockSpec((latp, lats), lambda q, o: (0, 0)),
            ],
            out_specs=[
                pl.BlockSpec((lats, rows, 2 * chan), lambda q, o: (0, 0, 0)),
                pl.BlockSpec((nbp, bs, lats), lambda q, o: (q, 0, 0)),
            ],
            scratch_shapes=[pltpu.VMEM((2, lats * stride, chan), F32)],
        ),
        out_shape=[
            jax.ShapeDtypeStruct((lats, rows, 2 * chan), BF),
            jax.ShapeDtypeStruct((pairs * nbp, bs, lats), BF),
        ],
        compiler_params=params(58),
        cost_estimate=pl.CostEstimate(
            flops=lats * 90 * 10**6, bytes_accessed=20 * 10**6 + lats * 10**5, transcendentals=0
        ),
        name="inverse_legendre",
    )(owners, leg, spec, order)


def fourier_kernel(chan, table_ref, turned_ref, recv_ref, prev_ref, grid_ref, send_ref):
    groups, _, rows, cols = recv_ref.shape
    total = groups * rows
    f = recv_ref[:, 0].reshape(total, cols)
    nlon = table_ref.shape[0]
    step = nlon // 4
    fluxes = []
    for w in range(4):
        values = dot(table_ref[w * step:(w + 1) * step], f, ((1,), (0,)))
        parts = []
        for h in range(2):
            x = values[:, h * chan:(h + 1) * chan]
            grid_ref[0, h, w * step:(w + 1) * step, :] = x.astype(BF)
            y = pltpu.roll(x, chan // 2, 1)
            lane = lax.broadcasted_iota(jnp.int32, x.shape, 1)
            parts.append(jnp.where(lane < chan // 2, x * y, 0.5 * (y * y - x * x)).astype(BF))
        fluxes.append(jnp.concatenate(parts, axis=1))
    flux = jnp.concatenate(fluxes, axis=0)
    coeffs = dot(turned_ref[...], flux, ((1,), (0,))).astype(BF)
    send_ref[:, 0] = coeffs.reshape(groups, rows, cols)


def fourier(table, turned, recv, prev, start, grid_shape):
    groups, lats, rows, cols = recv.shape
    nlon, total = table.shape
    chan = cols // 2
    whole = pl.BlockSpec((nlon, total), lambda t: (0, 0))
    turned_spec = pl.BlockSpec((total, nlon), lambda t: (0, 0))
    part = pl.BlockSpec((groups, 1, rows, cols), lambda t: (0, t, 0, 0))
    in_specs = [whole, turned_spec, part]
    args = [table, turned, recv]
    kernel = functools.partial(fourier_kernel, chan)
    alias = {}
    if prev is None:
        def kernel(a, b, c, d, e):
            fourier_kernel(chan, a, b, c, None, d, e)
    else:
        in_specs.append(pl.BlockSpec(memory_space=pl.ANY))
        args.append(prev)
        alias = {3: 0}
    return pl.pallas_call(
        kernel,
        grid=(lats,),
        in_specs=in_specs,
        out_specs=[
            pl.BlockSpec((1, 2, nlon, chan), lambda t: (start + t, 0, 0, 0)),
            part,
        ],
        out_shape=[
            jax.ShapeDtypeStruct(grid_shape, BF),
            jax.ShapeDtypeStruct(recv.shape, BF),
        ],
        input_output_aliases=alias,
        compiler_params=params(56),
        cost_estimate=pl.CostEstimate(flops=4 * lats * nlon * total * cols, bytes_accessed=20 * 10**6, transcendentals=0),
        name="fourier_step",
    )(*args)


def direct_kernel(dims, first, last, owners_ref, leg_ref, gauss_ref, got_ref, *rest):
    nbp, bs, nb, m_count, rows, stride, chan = dims
    prev_ref = None if first else rest[0]
    out_ref, acc_ref = rest[-2:]
    q = pl.program_id(0)
    half = bs // 2
    p = owners_ref[q]
    lats = got_ref.shape[0]

    @pl.when(q == 0)
    def _():
        def move(i, _):
            for h in range(2):
                full = got_ref[pl.ds(i * 16, 16), :, h * chan:(h + 1) * chan].astype(F32)
                if stride != rows:
                    full = jnp.concatenate([full, jnp.zeros((16, stride - rows, chan), F32)], axis=1)
                acc_ref[h, pl.ds(i * 16 * stride, 16 * stride), :] = full.reshape(16 * stride, chan)
            return 0

        lax.fori_loop(0, lats // 16, move, 0)

    g = gauss_ref[...]
    syms, antis = [], []
    for x in range(4):
        north = acc_ref[0, pl.ds(q * 4 + x, lats, stride=stride), :]
        south = acc_ref[1, pl.ds(q * 4 + x, lats, stride=stride), :]
        syms.append((g * (north + south)).astype(BF))
        antis.append((g * (north - south)).astype(BF))
    te = jnp.concatenate([leg_ref[j, :half] for j in range(nbp)], axis=0)
    to = jnp.concatenate([leg_ref[j, half:] for j in range(nbp)], axis=0)
    even = dot(te, jnp.concatenate(syms, axis=1), ((1,), (0,)))
    odd = dot(to, jnp.concatenate(antis, axis=1), ((1,), (0,)))
    for j in range(nbp):
        both = jnp.concatenate([even[j * half:(j + 1) * half], odd[j * half:(j + 1) * half]], axis=0)
        shape = (bs, 2 * chan)
        lead, live = block_facts(p, j, nb, bs, m_count, (bs, 1))
        one = lead.astype(jnp.int32)
        pick = jnp.where(jnp.broadcast_to(one, shape) == 1, both[:, :2 * chan], both[:, 2 * chan:])
        if not first:
            pick = pick + prev_ref[j]
        if last:
            pick = pick * live.astype(F32)
        out_ref[j] = pick.astype(out_ref.dtype)


def direct(owners, leg, gauss, got, prev, dims, last):
    nbp, bs, nb, m_count, rows, stride, chan = dims
    pairs = owners.shape[0]
    lats = got.shape[0]
    blocks = pl.BlockSpec((nbp, bs, 2 * chan), lambda q, o: (q, 0, 0))
    in_specs = [
        pl.BlockSpec((nbp, bs, lats), lambda q, o: (q, 0, 0)),
        pl.BlockSpec((lats, chan), lambda q, o: (0, 0)),
        pl.BlockSpec((lats, rows, 2 * chan), lambda q, o: (0, 0, 0)),
    ]
    args = [owners, leg, gauss, got]
    alias = {}
    if prev is not None:
        in_specs.append(blocks)
        args.append(prev)
        if not last:
            alias = {4: 0}
    return pl.pallas_call(
        functools.partial(direct_kernel, dims, prev is None, last),
        grid_spec=pltpu.PrefetchScalarGridSpec(
            num_scalar_prefetch=1,
            grid=(pairs,),
            in_specs=in_specs,
            out_specs=blocks,
            scratch_shapes=[pltpu.VMEM((2, lats * stride, chan), F32)],
        ),
        out_shape=jax.ShapeDtypeStruct((pairs * nbp, bs, 2 * chan), BF if last else F32),
        input_output_aliases=alias,
        compiler_params=params(58),
        cost_estimate=pl.CostEstimate(
            flops=lats * 40 * 10**6, bytes_accessed=25 * 10**6 + lats * 10**5, transcendentals=0
        ),
        name="direct_legendre",
    )(*args)


def fourier_basis(pair_ids, m_count, nlon):
    wave = jnp.stack([pair_ids, m_count - 1 - pair_ids], axis=1).reshape(m_count, 1)
    longitude = jnp.arange(nlon, dtype=jnp.int32)[None, :]
    angles = (longitude * wave % nlon).astype(F32) * (2.0 * math.pi / nlon)
    scaled = jnp.stack([jnp.cos(angles), -jnp.sin(angles)], axis=1) * (1.0 / math.sqrt(m_count))
    return scaled.astype(BF).reshape(2 * m_count, nlon)


def per_device(spectrum, owners, legendre, gauss_weights):
    pairs = owners.shape[0]
    devices = lax.axis_size("lat")
    blocks, bs, cols = spectrum.shape
    nbp = blocks // pairs
    nb = nbp - 1
    chan = cols // 2
    m_count = 2 * pairs * devices
    nlon = 2 * m_count
    latp = legendre.shape[2]
    here = latp // devices
    fifth = here // 5
    sizes = (fifth, 3 * fifth, fifth) if here % 5 == 0 else (here,)
    starts = [sum(sizes[:c]) for c in range(len(sizes))]
    rows = 4 * pairs
    stride = -(-rows // 16) * 16
    dims = (nbp, bs, nb, m_count, rows, stride, chan)
    aligned = rows % 16 == 0
    grid_shape = (here, 2, nlon, chan)

    copies = jnp.broadcast_to(owners[None, :], (devices, pairs))
    all_owners = lax.all_to_all(copies, "lat", split_axis=0, concat_axis=0, tiled=True).reshape(-1)

    def swap(x):
        return lax.all_to_all(x, "lat", split_axis=0, concat_axis=0, tiled=True)

    def places(c):
        device = jnp.arange(devices, dtype=jnp.int32)[:, None]
        return (device * here + starts[c] + jnp.arange(sizes[c], dtype=jnp.int32)[None, :]).reshape(-1)

    def inverse_chunk(c):
        order = (jnp.arange(latp, dtype=jnp.int32)[:, None] == places(c)[None, :]).astype(BF)
        out, leg = inverse(owners, legendre, spectrum, order, dims)
        return out.reshape(devices, sizes[c], rows, cols), leg

    def fourier_chunk(c, got, grid):
        if not aligned:
            got = got.transpose(1, 0, 2, 3).reshape(1, sizes[c], devices * rows, cols)
        grid, send = fourier(table, turned, got, grid, starts[c], grid_shape)
        if not aligned:
            send = send.reshape(sizes[c], devices, rows, cols).transpose(1, 0, 2, 3)
        return grid, send

    count = len(sizes)
    outs, legs = zip(*[inverse_chunk(c) for c in range(count)])
    outs = list(outs)
    outs[0], all_owners = lax.optimization_barrier((outs[0], all_owners))
    received = [swap(outs[0])]
    turned = fourier_basis(all_owners, m_count, nlon)
    table = turned.T
    grid, send = fourier_chunk(0, received[0], None)
    sends = [send]
    for c in range(1, count):
        if c == 2:
            outs[c], sends[0], grid = lax.optimization_barrier((outs[c], sends[0], grid))
        received.append(swap(outs[c]))
        if c == 1:
            sends[0], received[1] = lax.optimization_barrier((sends[0], received[1]))
    for c in range(1, count):
        grid, send = fourier_chunk(c, received[c], grid)
        sends.append(send)
    tendency = None
    for c in range(count):
        got = swap(sends[c]).reshape(devices * sizes[c], rows, cols)
        gauss = jnp.broadcast_to(
            gauss_weights.reshape(devices, here)[:, starts[c]:starts[c] + sizes[c]].reshape(-1, 1),
            (devices * sizes[c], chan),
        )
        tendency = direct(owners, legs[c], gauss, got, tendency, dims, c == count - 1)
    return grid, tendency


def solution(mesh):
    in_specs = (P(("grp", "lat"), None, None), P("lat"), P("lat", None, None), P())
    out_specs = (P(("grp", "lat"), None, None, None), P(("grp", "lat"), None, None))
    return jax.shard_map(
        per_device, mesh=mesh, in_specs=in_specs, out_specs=out_specs, check_vma=False
    )
```
